32 devices in a mesh: inp: 4 (over z), wt: 4 (over y, x), out: 2 (over core).
Axes of the slice: x: 2, y: 2, z: 4, core: 2. Of those that a mesh axis runs over, the one named last changes fastest.
Arguments:
- tokens: bfloat16 [256, 16384], P(('wt', 'out'), 'inp'), may hold values from -6 to 6
- gate_weight: bfloat16 [16384, 26624], P('inp', ('wt', 'out')), may hold values from -0.046875 to 0.046875
- up_weight: bfloat16 [16384, 26624], P('inp', ('wt', 'out')), may hold values from -0.046875 to 0.046875
- hidden_grad: bfloat16 [256, 26624], P('inp', ('wt', 'out')), may hold values from -1.5 to 1.5
Outputs:
- input_grad: bfloat16 [256, 16384], P(('wt', 'out'), 'inp')
- gate_grad: bfloat16 [16384, 26624], P('inp', ('wt', 'out'))
- up_grad: bfloat16 [16384, 26624], P('inp', ('wt', 'out'))
The draws below stay inside these ranges and needn't reach their ends.
All inputs are finite; a program needn't handle non-finite values.
Results may differ from the reference program's by a relative error of at most 0.0049.
Values may be sent and summed in bfloat16 or wider, within the bound.
A program may use at most 192 MiB of HBM per device.

```python
import jax
import jax.numpy as jnp
from jax import lax

D = 16384
F = 26624
TOKENS = 256


def levels(rng, shape, split, least, high):
    def one(axis_at, parts):
        draws = jax.random.uniform(jax.random.fold_in(jax.random.fold_in(rng, 6), axis_at), (parts,), jnp.float32, least / len(split), high / len(split))
        return jnp.repeat(jnp.exp(draws), shape[axis_at] // parts).reshape((-1,) + (1,) * (len(shape) - axis_at - 1))

    level = one(*split[0])
    for cut in split[1:]:
        level = level * one(*cut)
    return level


def centred(own_key, shape, deviation, limit, shards=(), kind=jnp.bfloat16):
    entries = deviation * jax.random.normal(own_key, shape, jnp.float32)
    if shards:
        entries = entries * levels(own_key, shape, shards, -0.22, 0.18)
    return jnp.clip(entries, -limit, limit).astype(kind)


def setup_inputs(seed: int = 0) -> dict:
    key_of = jax.random.split(jax.random.key(seed), 5)
    tokens = centred(key_of[0], (TOKENS, D), 1.0, 6.0, ((0, 8), (1, 4)))
    gate_weight = centred(key_of[1], (D, F), D ** -0.5, 0.046875, ((0, 4), (1, 8)))
    up_weight = centred(key_of[2], (D, F), D ** -0.5, 0.046875, ((0, 4), (1, 8)))
    hidden_grad = centred(key_of[3], (TOKENS, F), 0.25, 1.5, ((0, 4), (1, 8)))
    return {"tokens": tokens, "gate_weight": gate_weight, "up_weight": up_weight, "hidden_grad": hidden_grad}


def deltas(gate_act, up_act, grad):
    logistic = jax.nn.sigmoid(gate_act)
    up_delta = (grad * (gate_act * logistic)).astype(jnp.bfloat16)
    gate_delta = (grad * up_act * logistic * (1.0 + gate_act * (1.0 - logistic))).astype(jnp.bfloat16)
    return gate_delta, up_delta


def reference(tokens, gate_weight, up_weight, hidden_grad):
    block = F // 16
    features = tokens.astype(jnp.float32)
    highest = lax.Precision.HIGHEST

    def step(carry, index):
        first = (index * block).astype(jnp.int32)
        gate_cols = lax.dynamic_slice_in_dim(gate_weight, first, block, 1).astype(jnp.float32)
        up_cols = lax.dynamic_slice_in_dim(up_weight, first, block, 1).astype(jnp.float32)
        grad_cols = lax.dynamic_slice_in_dim(hidden_grad, first, block, 1).astype(jnp.float32)
        gate_act = jnp.dot(features, gate_cols, precision=highest)
        up_act = jnp.dot(features, up_cols, precision=highest)
        gate_delta, up_delta = deltas(gate_act, up_act, grad_cols)
        gate_part = gate_delta.astype(jnp.float32)
        up_part = up_delta.astype(jnp.float32)
        gate_block = jnp.dot(features.T, gate_part, precision=highest).astype(jnp.bfloat16)
        up_block = jnp.dot(features.T, up_part, precision=highest).astype(jnp.bfloat16)
        carry = carry + jnp.dot(gate_part, gate_cols.T, precision=highest) + jnp.dot(up_part, up_cols.T, precision=highest)
        return carry, (gate_block, up_block)

    start_carry = jnp.zeros((TOKENS, D), jnp.float32)
    total, (gate_blocks, up_blocks) = lax.scan(step, start_carry, jnp.arange(16, dtype=jnp.int32))
    gate_grad = jnp.moveaxis(gate_blocks, 0, 1).reshape(D, F)
    up_grad = jnp.moveaxis(up_blocks, 0, 1).reshape(D, F)
    return total.astype(jnp.bfloat16), gate_grad, up_grad
```

```python
import jax
import jax.numpy as jnp
from jax import lax
from jax.experimental import pallas as pl
from jax.experimental.pallas import tpu as pltpu
from jax.sharding import PartitionSpec as P

OVER_TOKENS = (((0,), (0,)), ((), ()))
OVER_HIDDEN = (((1,), (1,)), ((), ()))


def deltas(gate_act, up_act, grad):
    logistic = jax.nn.sigmoid(gate_act)
    up_delta = (grad * (gate_act * logistic)).astype(jnp.bfloat16)
    gate_delta = (grad * up_act * logistic * (1.0 + gate_act * (1.0 - logistic))).astype(
        jnp.bfloat16
    )
    return (gate_delta, up_delta)


def grads_kernel(features, gate_delta, up_delta, gate_grad, up_grad):
    for delta, grad in ((gate_delta, gate_grad), (up_delta, up_grad)):
        grad[...] = lax.dot_general(
            features[...], delta[...], OVER_TOKENS, preferred_element_type=jnp.float32
        ).astype(jnp.bfloat16)


def weight_grads(features, gate_delta, up_delta):
    tokens, width = features.shape
    hidden = gate_delta.shape[1]
    rows = 256
    grad = jax.ShapeDtypeStruct((width, hidden), jnp.bfloat16)
    return pl.pallas_call(
        grads_kernel,
        grid=(width // rows,),
        in_specs=[
            pl.BlockSpec((tokens, rows), lambda i: (0, i)),
            pl.BlockSpec((tokens, hidden), lambda i: (0, 0)),
            pl.BlockSpec((tokens, hidden), lambda i: (0, 0)),
        ],
        out_specs=[pl.BlockSpec((rows, hidden), lambda i: (i, 0))] * 2,
        out_shape=[grad, grad],
        compiler_params=pltpu.CompilerParams(vmem_limit_bytes=40 * 2**20),
        cost_estimate=pl.CostEstimate(
            flops=4 * tokens * width * hidden,
            bytes_accessed=4 * width * hidden,
            transcendentals=0,
        ),
    )(features, gate_delta, up_delta)


def per_device(tokens, gate_weight, up_weight, hidden_grad):
    features = lax.all_gather(tokens, ("wt", "out"), axis=0, tiled=True)
    gate_act = jnp.dot(features, gate_weight, preferred_element_type=jnp.float32)
    up_act = jnp.dot(features, up_weight, preferred_element_type=jnp.float32)
    gate_act, up_act = lax.psum_scatter(
        (gate_act, up_act), "inp", scatter_dimension=0, tiled=True
    )
    gate_delta, up_delta = deltas(gate_act, up_act, hidden_grad.astype(jnp.float32))
    gate_delta, up_delta = lax.all_gather((gate_delta, up_delta), "inp", axis=0, tiled=True)
    first = lax.dot_general(
        gate_delta, gate_weight, OVER_HIDDEN, preferred_element_type=jnp.float32
    )
    summed = lax.psum_scatter(
        first
        + lax.dot_general(up_delta, up_weight, OVER_HIDDEN, preferred_element_type=jnp.float32),
        ("wt", "out"),
        scatter_dimension=0,
        tiled=True,
    )
    gate_grad, up_grad = weight_grads(features, gate_delta, up_delta)
    return (summed.astype(jnp.bfloat16), gate_grad, up_grad)


def solution(mesh):
    return jax.shard_map(
        per_device,
        mesh=mesh,
        in_specs=(
            P(("wt", "out"), "inp"),
            P("inp", ("wt", "out")),
            P("inp", ("wt", "out")),
            P("inp", ("wt", "out")),
        ),
        out_specs=(P(("wt", "out"), "inp"), P("inp", ("wt", "out")), P("inp", ("wt", "out"))),
        check_vma=False,
    )
```

```python
import functools

import jax
import jax.numpy as jnp
from jax import lax
from jax.experimental import pallas as pl
from jax.experimental.pallas import tpu as pltpu
from jax.sharding import PartitionSpec as P

OVER_TOKENS = (((0,), (0,)), ((), ()))
OVER_HIDDEN = (((1,), (1,)), ((), ()))


def deltas(gate_act, up_act, grad):
    logistic = jax.nn.sigmoid(gate_act)
    up_delta = (grad * (gate_act * logistic)).astype(jnp.bfloat16)
    gate_delta = (grad * up_act * logistic * (1.0 + gate_act * (1.0 - logistic))).astype(
        jnp.bfloat16
    )
    return (gate_delta, up_delta)


def grads_kernel(features, gate_delta, up_delta, gate_grad, up_grad):
    for delta, grad in ((gate_delta, gate_grad), (up_delta, up_grad)):
        grad[...] = lax.dot_general(
            features[...], delta[...], OVER_TOKENS, preferred_element_type=jnp.float32
        ).astype(jnp.bfloat16)


def weight_grads(features, gate_delta, up_delta):
    tokens, width = features.shape
    hidden = gate_delta.shape[1]
    rows = 256
    grad = jax.ShapeDtypeStruct((width, hidden), jnp.bfloat16)
    return pl.pallas_call(
        grads_kernel,
        grid=(width // rows,),
        in_specs=[
            pl.BlockSpec((tokens, rows), lambda i: (0, i)),
            pl.BlockSpec((tokens, hidden), lambda i: (0, 0)),
            pl.BlockSpec((tokens, hidden), lambda i: (0, 0)),
        ],
        out_specs=[pl.BlockSpec((rows, hidden), lambda i: (i, 0))] * 2,
        out_shape=[grad, grad],
        compiler_params=pltpu.CompilerParams(vmem_limit_bytes=40 * 2**20),
        cost_estimate=pl.CostEstimate(
            flops=4 * tokens * width * hidden,
            bytes_accessed=4 * width * hidden,
            transcendentals=0,
        ),
    )(features, gate_delta, up_delta)


def per_device(tokens, gate_weight, up_weight, hidden_grad):
    features = lax.all_gather(tokens, ("wt", "out"), axis=0, tiled=True)
    gate_act = jnp.dot(features, gate_weight, preferred_element_type=jnp.float32)
    up_act = jnp.dot(features, up_weight, preferred_element_type=jnp.float32)
    gate_act, up_act = lax.psum_scatter(
        (gate_act, up_act), "inp", scatter_dimension=0, tiled=True
    )
    gate_delta, up_delta = deltas(gate_act, up_act, hidden_grad.astype(jnp.float32))
    gate_delta, up_delta = lax.all_gather((gate_delta, up_delta), "inp", axis=0, tiled=True)
    first = lax.dot_general(
        gate_delta, gate_weight, OVER_HIDDEN, preferred_element_type=jnp.float32
    )
    summed = lax.psum_scatter(
        first
        + lax.dot_general(up_delta, up_weight, OVER_HIDDEN, preferred_element_type=jnp.float32),
        ("wt", "out"),
        scatter_dimension=0,
        tiled=True,
    )
    gate_grad, up_grad = weight_grads(features, gate_delta, up_delta)
    return (summed.astype(jnp.bfloat16), gate_grad, up_grad)


MESH = pl.DeviceIdType.MESH
CHUNK = 256
SUM_LAG, DELTA_LAG, MID_LAG, EDGE_LAG = 1, 3, 4, 6


def exchange_kernel(
    chunks,
    tokens, hidden, gate_weight, up_weight,
    input_grad, features_out, delta_out,
    features, grads, forward_w, backward_w, acts_out, from_edge, from_mid, delta, own, total,
    pair_in, plane_out, plane_in,
    gather_send, gather_recv, relay_send, relay_recv, grad_send, grad_recv,
    forward_sem, backward_sem, act_send, edge_recv, mid_recv, delta_send, delta_recv,
    pair_send, pair_recv, plane_send, plane_recv, out_sem,
):
    z, wt, out = lax.axis_index("inp"), lax.axis_index("wt"), lax.axis_index("out")
    rows, width = tokens.shape
    chunk_rows = hidden.shape[0]
    is_mid = jnp.logical_and(z > 0, z < 3)
    is_edge = jnp.logical_not(is_mid)
    paired = z + 1 - 2 * lax.rem(z, 2)
    other_mid = 3 - z
    plane = (None, wt + 1 - 2 * lax.rem(wt, 2), lax.rem(wt + 2, 4), 3 - wt)
    core = {"out": 1 - out}

    def remote(src, dst, send, recv, to):
        return pltpu.make_async_remote_copy(
            src_ref=src, dst_ref=dst, send_sem=send, recv_sem=recv,
            device_id=to, device_id_type=MESH,
        )

    def weight_copies(c, slots, sems):
        slot = lax.rem(c, 2)
        columns = pl.ds(pl.multiple_of(c * CHUNK, CHUNK), CHUNK)
        return [
            pltpu.make_async_copy(
                w.at[:, columns], slots.at[slot, :, pl.ds(i * CHUNK, CHUNK)], sems.at[slot, i]
            )
            for i, w in enumerate((gate_weight, up_weight))
        ]

    for c in range(2):
        for copy in weight_copies(c, forward_w, forward_sem):
            copy.start()
        for copy in weight_copies(c, backward_w, backward_sem):
            copy.start()

    barrier = pltpu.get_barrier_semaphore()
    for k in (1, 2, 3):
        pl.semaphore_signal(barrier, inc=1, device_id={"wt": plane[k]}, device_id_type=MESH)
    pl.semaphore_signal(barrier, inc=1, device_id=core, device_id_type=MESH)
    pl.semaphore_signal(barrier, inc=1, device_id={"inp": paired}, device_id_type=MESH)

    @pl.when(is_mid)
    def _():
        pl.semaphore_signal(barrier, inc=1, device_id={"inp": other_mid}, device_id_type=MESH)
        pl.semaphore_wait(barrier, 6)

    @pl.when(is_edge)
    def _():
        pl.semaphore_wait(barrier, 5)

    def block(w, o):
        return pl.ds(pl.multiple_of((w * 2 + o) * rows, rows), rows)

    mine = block(wt, out)
    gathers = [remote(tokens, features.at[mine], gather_send.at[0], gather_recv.at[0], core)]
    for k in (3, 1, 2):
        gathers.append(
            remote(tokens, features.at[mine], gather_send.at[k], gather_recv.at[k], {"wt": plane[k]})
        )
    for copy in gathers:
        copy.start()

    @pl.when(is_edge)
    def _():
        remote(hidden, grads.at[z], grad_send.at[0], grad_recv.at[0], {"inp": paired}).start()

    @pl.when(is_mid)
    def _():
        remote(hidden, grads.at[z], grad_send.at[0], grad_recv.at[1], {"inp": other_mid}).start()
        grads[z] = hidden[...]

    features[mine, :] = tokens[...]
    total[...] = jnp.zeros_like(total)

    relays = []
    for k in (1, 2, 3):
        theirs = block(plane[k], out)
        remote(
            tokens, features.at[theirs], gather_send.at[k], gather_recv.at[k], {"wt": plane[k]}
        ).wait_recv()
        relay = remote(
            features.at[theirs], features.at[theirs], relay_send.at[k], relay_recv.at[k], core
        )
        relay.start()
        relays.append(relay)

    def relayed_grads():
        return remote(
            grads.at[paired], grads.at[paired], grad_send.at[1], grad_recv.at[2], {"inp": other_mid}
        )

    @pl.when(is_mid)
    def _():
        remote(
            hidden, grads.at[paired], grad_send.at[0], grad_recv.at[0], {"inp": paired}
        ).wait_recv()
        relayed_grads().start()

    remote(
        tokens, features.at[block(wt, 1 - out)], gather_send.at[0], gather_recv.at[0], core
    ).wait_recv()
    for k in (1, 2, 3):
        theirs = block(plane[k], 1 - out)
        remote(
            features.at[theirs], features.at[theirs], relay_send.at[k], relay_recv.at[k], core
        ).wait_recv()
    features_copy = pltpu.make_async_copy(features, features_out, out_sem.at[0])
    features_copy.start()

    def edge_copy(c):
        return remote(
            acts_out.at[c], from_edge.at[c], act_send.at[c], edge_recv.at[c], {"inp": paired}
        )

    def mid_copy(c):
        return remote(
            acts_out.at[c], from_mid.at[c], act_send.at[c], mid_recv.at[c], {"inp": other_mid}
        )

    def delta_copy(c):
        return remote(
            delta.at[c], delta.at[c], delta_send.at[c], delta_recv.at[c], {"inp": paired}
        )

    def step(t, carry):
        @pl.when(t < chunks)
        def _():
            for copy in weight_copies(t, forward_w, forward_sem):
                copy.wait()
            partial = jnp.dot(
                features[...], forward_w[lax.rem(t, 2)], preferred_element_type=jnp.float32
            )

            @pl.when(is_edge)
            def _():
                acts_out[t] = partial.astype(jnp.bfloat16)
                edge_copy(t).start()

            @pl.when(is_mid)
            def _():
                own[t] = partial

            @pl.when(t + 2 < chunks)
            def _():
                for copy in weight_copies(t + 2, forward_w, forward_sem):
                    copy.start()

        c1 = t - SUM_LAG

        @pl.when(is_mid & (c1 >= 0) & (c1 < chunks))
        def _():
            edge_copy(c1).wait_recv()
            both = own[c1] + from_edge[c1].astype(jnp.float32)
            own[c1] = both
            acts_out[c1] = both.astype(jnp.bfloat16)
            mid_copy(c1).start()

        c2 = t - DELTA_LAG

        @pl.when(is_mid & (c2 == 0))
        def _():
            remote(
                hidden, grads.at[other_mid], grad_send.at[0], grad_recv.at[1], {"inp": other_mid}
            ).wait_recv()
            far = 3 - paired
            remote(
                grads.at[far], grads.at[far], grad_send.at[1], grad_recv.at[2], {"inp": other_mid}
            ).wait_recv()

        @pl.when(is_mid & (c2 >= 0) & (c2 < chunks))
        def _():
            mid_copy(c2).wait_recv()
            columns = pl.ds(pl.multiple_of(c2 * CHUNK, CHUNK), CHUNK)
            for q in range(4):
                part = pl.ds(q * chunk_rows, chunk_rows)
                acts = own[c2, part, :] + from_mid[c2, part, :].astype(jnp.float32)
                gate_delta, up_delta = deltas(
                    acts[:, :CHUNK], acts[:, CHUNK:], grads[q, :, columns].astype(jnp.float32)
                )
                delta[c2, part, pl.ds(0, CHUNK)] = gate_delta
                delta[c2, part, pl.ds(CHUNK, CHUNK)] = up_delta
            delta_copy(c2).start()

        cb = t - jnp.where(is_mid, MID_LAG, EDGE_LAG)

        @pl.when((cb >= 0) & (cb < chunks))
        def _():
            @pl.when(is_edge)
            def _():
                delta_copy(cb).wait_recv()

            for copy in weight_copies(cb, backward_w, backward_sem):
                copy.wait()
            slot = lax.rem(cb, 2)

            def piece(i, carry):
                at = pl.ds(pl.multiple_of(i * 512, 512), 512)
                total[:, at] += lax.dot_general(
                    delta[cb], backward_w[slot, at, :], OVER_HIDDEN,
                    preferred_element_type=jnp.float32,
                )
                return carry

            lax.fori_loop(0, width // 512, piece, 0)

            @pl.when(cb + 2 < chunks)
            def _():
                for copy in weight_copies(cb + 2, backward_w, backward_sem):
                    copy.start()

        return carry

    lax.fori_loop(0, chunks + EDGE_LAG, step, 0)
    delta_out_copy = pltpu.make_async_copy(delta, delta_out, out_sem.at[1])
    delta_out_copy.start()

    targets = (wt,) + plane[1:]

    def pair_copy(k, o):
        return remote(
            total.at[block(targets[k], o)], pair_in.at[k], pair_send.at[k], pair_recv.at[k], core
        )

    for k in (3, 1, 2, 0):
        pair_copy(k, 1 - out).start()
    for k in (3, 1, 2):
        pair_copy(k, 1 - out).wait_recv()
        plane_out[k - 1] = (total[block(targets[k], out), :] + pair_in[k]).astype(jnp.bfloat16)
        remote(
            plane_out.at[k - 1], plane_in.at[k - 1], plane_send.at[k], plane_recv.at[k],
            {"wt": plane[k]},
        ).start()
    pair_copy(0, 1 - out).wait_recv()
    result = total[mine, :] + pair_in[0]
    for k in (1, 2, 3):
        copy = remote(
            plane_out.at[k - 1], plane_in.at[k - 1], plane_send.at[k], plane_recv.at[k],
            {"wt": plane[k]},
        )
        copy.wait_recv()
        result = result + plane_in[k - 1].astype(jnp.float32)
        copy.wait_send()
    input_grad[...] = result.astype(jnp.bfloat16)

    for k in range(4):
        pair_copy(k, 1 - out).wait_send()
    for copy in gathers + relays:
        copy.wait_send()
    remote(hidden, grads.at[z], grad_send.at[0], grad_recv.at[0], {"inp": paired}).wait_send()

    @pl.when(is_mid)
    def _():
        relayed_grads().wait_send()

    def finish(c, carry):
        edge_copy(c).wait_send()

        @pl.when(is_mid)
        def _():
            delta_copy(c).wait_send()

        return carry

    lax.fori_loop(0, chunks, finish, 0)
    features_copy.wait()
    delta_out_copy.wait()


def exchange(tokens, gate_weight, up_weight, hidden_grad):
    rows, width = tokens.shape
    hidden = gate_weight.shape[1]
    chunks = hidden // CHUNK
    whole = rows * 8
    bf16, f32 = jnp.bfloat16, jnp.float32
    dma = pltpu.SemaphoreType.DMA
    vmem, hbm = pl.BlockSpec(memory_space=pltpu.VMEM), pl.BlockSpec(memory_space=pl.ANY)
    acts = (chunks, whole, 2 * CHUNK)
    return pl.pallas_call(
        functools.partial(exchange_kernel, chunks),
        out_shape=(
            jax.ShapeDtypeStruct((rows, width), bf16),
            jax.ShapeDtypeStruct((whole, width), bf16),
            jax.ShapeDtypeStruct(acts, bf16),
        ),
        in_specs=[vmem, vmem, hbm, hbm],
        out_specs=(vmem, hbm, hbm),
        scratch_shapes=[
            pltpu.VMEM((whole, width), bf16),
            pltpu.VMEM((4, whole // 4, hidden), bf16),
            pltpu.VMEM((2, width, 2 * CHUNK), bf16),
            pltpu.VMEM((2, width, 2 * CHUNK), bf16),
            pltpu.VMEM(acts, bf16),
            pltpu.VMEM(acts, bf16),
            pltpu.VMEM(acts, bf16),
            pltpu.VMEM(acts, bf16),
            pltpu.VMEM(acts, f32),
            pltpu.VMEM((whole, width), f32),
            pltpu.VMEM((4, rows, width), f32),
            pltpu.VMEM((3, rows, width), bf16),
            pltpu.VMEM((3, rows, width), bf16),
            dma((4,)), dma((4,)), dma((4,)), dma((4,)), dma((2,)), dma((3,)),
            dma((2, 2)), dma((2, 2)),
            dma((chunks,)), dma((chunks,)), dma((chunks,)), dma((chunks,)), dma((chunks,)),
            dma((4,)), dma((4,)), dma((4,)), dma((4,)), dma((2,)),
        ],
        compiler_params=pltpu.CompilerParams(
            collective_id=0, has_side_effects=True, vmem_limit_bytes=58 * 2**20
        ),
        cost_estimate=pl.CostEstimate(
            flops=8 * whole * width * hidden,
            bytes_accessed=8 * width * hidden,
            transcendentals=whole * hidden,
        ),
    )(tokens, hidden_grad, gate_weight, up_weight)


def chunk_grads_kernel(features, delta, gate_grad, up_grad):
    turned = features[...].T
    for c in range(delta.shape[0]):
        both = jnp.dot(turned, delta[c], preferred_element_type=jnp.float32).astype(jnp.bfloat16)
        at = pl.ds(c * CHUNK, CHUNK)
        gate_grad[:, at] = both[:, :CHUNK]
        up_grad[:, at] = both[:, CHUNK:]


def chunk_grads(features, delta):
    tokens, width = features.shape
    chunks = delta.shape[0]
    hidden = chunks * CHUNK
    rows = 256
    grad = jax.ShapeDtypeStruct((width, hidden), jnp.bfloat16)
    return pl.pallas_call(
        chunk_grads_kernel,
        grid=(width // rows,),
        in_specs=[
            pl.BlockSpec((tokens, rows), lambda i: (0, i)),
            pl.BlockSpec(delta.shape, lambda i: (0, 0, 0)),
        ],
        out_specs=[pl.BlockSpec((rows, hidden), lambda i: (i, 0))] * 2,
        out_shape=[grad, grad],
        compiler_params=pltpu.CompilerParams(vmem_limit_bytes=40 * 2**20),
        cost_estimate=pl.CostEstimate(
            flops=4 * tokens * width * hidden,
            bytes_accessed=4 * width * hidden,
            transcendentals=0,
        ),
    )(features, delta)


def on_line(tokens, gate_weight, up_weight, hidden_grad):
    input_grad, features, delta = exchange(tokens, gate_weight, up_weight, hidden_grad)
    gate_grad, up_grad = chunk_grads(features, delta)
    return (input_grad, gate_grad, up_grad)


def solution(mesh):
    line = (mesh.shape["inp"], mesh.shape["wt"], mesh.shape["out"]) == (4, 4, 2)
    return jax.shard_map(
        on_line if line else per_device,
        mesh=mesh,
        in_specs=(
            P(("wt", "out"), "inp"),
            P("inp", ("wt", "out")),
            P("inp", ("wt", "out")),
            P("inp", ("wt", "out")),
        ),
        out_specs=(P(("wt", "out"), "inp"), P("inp", ("wt", "out")), P("inp", ("wt", "out"))),
        check_vma=False,
    )
```

```python
import functools

import jax
import jax.numpy as jnp
from jax import lax
from jax.experimental import pallas as pl
from jax.experimental.pallas import tpu as pltpu
from jax.sharding import PartitionSpec as P

OVER_TOKENS = (((0,), (0,)), ((), ()))
OVER_HIDDEN = (((1,), (1,)), ((), ()))


def deltas(gate_act, up_act, grad):
    logistic = jax.nn.sigmoid(gate_act)
    up_delta = (grad * (gate_act * logistic)).astype(jnp.bfloat16)
    gate_delta = (grad * up_act * logistic * (1.0 + gate_act * (1.0 - logistic))).astype(
        jnp.bfloat16
    )
    return (gate_delta, up_delta)


def grads_kernel(features, gate_delta, up_delta, gate_grad, up_grad):
    for delta, grad in ((gate_delta, gate_grad), (up_delta, up_grad)):
        grad[...] = lax.dot_general(
            features[...], delta[...], OVER_TOKENS, preferred_element_type=jnp.float32
        ).astype(jnp.bfloat16)


def weight_grads(features, gate_delta, up_delta):
    tokens, width = features.shape
    hidden = gate_delta.shape[1]
    rows = 256
    grad = jax.ShapeDtypeStruct((width, hidden), jnp.bfloat16)
    return pl.pallas_call(
        grads_kernel,
        grid=(width // rows,),
        in_specs=[
            pl.BlockSpec((tokens, rows), lambda i: (0, i)),
            pl.BlockSpec((tokens, hidden), lambda i: (0, 0)),
            pl.BlockSpec((tokens, hidden), lambda i: (0, 0)),
        ],
        out_specs=[pl.BlockSpec((rows, hidden), lambda i: (i, 0))] * 2,
        out_shape=[grad, grad],
        compiler_params=pltpu.CompilerParams(vmem_limit_bytes=40 * 2**20),
        cost_estimate=pl.CostEstimate(
            flops=4 * tokens * width * hidden,
            bytes_accessed=4 * width * hidden,
            transcendentals=0,
        ),
    )(features, gate_delta, up_delta)


def per_device(tokens, gate_weight, up_weight, hidden_grad):
    features = lax.all_gather(tokens, ("wt", "out"), axis=0, tiled=True)
    gate_act = jnp.dot(features, gate_weight, preferred_element_type=jnp.float32)
    up_act = jnp.dot(features, up_weight, preferred_element_type=jnp.float32)
    gate_act, up_act = lax.psum_scatter(
        (gate_act, up_act), "inp", scatter_dimension=0, tiled=True
    )
    gate_delta, up_delta = deltas(gate_act, up_act, hidden_grad.astype(jnp.float32))
    gate_delta, up_delta = lax.all_gather((gate_delta, up_delta), "inp", axis=0, tiled=True)
    first = lax.dot_general(
        gate_delta, gate_weight, OVER_HIDDEN, preferred_element_type=jnp.float32
    )
    summed = lax.psum_scatter(
        first
        + lax.dot_general(up_delta, up_weight, OVER_HIDDEN, preferred_element_type=jnp.float32),
        ("wt", "out"),
        scatter_dimension=0,
        tiled=True,
    )
    gate_grad, up_grad = weight_grads(features, gate_delta, up_delta)
    return (summed.astype(jnp.bfloat16), gate_grad, up_grad)


MESH = pl.DeviceIdType.MESH
CHUNK = 256
SUM_LAG, DELTA_LAG, MID_LAG, EDGE_LAG = 1, 2, 3, 8


def exchange_kernel(
    chunks,
    tokens, hidden, gate_weight, up_weight,
    input_grad, features_out, delta_out,
    features, grads, forward_w, backward_w, acts_out, from_edge, from_mid, delta, own, total,
    pair_in, plane_out, plane_in,
    gather_send, gather_recv, relay_send, relay_recv, grad_send, grad_recv,
    forward_sem, backward_sem, act_send, edge_recv, mid_recv, delta_send, delta_recv,
    pair_send, pair_recv, plane_send, plane_recv, out_sem,
):
    z, wt, out = lax.axis_index("inp"), lax.axis_index("wt"), lax.axis_index("out")
    rows, width = tokens.shape
    chunk_rows = hidden.shape[0]
    is_mid = jnp.logical_and(z > 0, z < 3)
    is_edge = jnp.logical_not(is_mid)
    paired = z + 1 - 2 * lax.rem(z, 2)
    other_mid = 3 - z
    plane = (None, wt + 1 - 2 * lax.rem(wt, 2), lax.rem(wt + 2, 4), 3 - wt)
    core = {"out": 1 - out}

    def remote(src, dst, send, recv, to):
        return pltpu.make_async_remote_copy(
            src_ref=src, dst_ref=dst, send_sem=send, recv_sem=recv,
            device_id=to, device_id_type=MESH,
        )

    def weight_copies(c, slots, sems):
        slot = lax.rem(c, 2)
        columns = pl.ds(pl.multiple_of(c * CHUNK, CHUNK), CHUNK)
        return [
            pltpu.make_async_copy(
                w.at[:, columns], slots.at[slot, :, pl.ds(i * CHUNK, CHUNK)], sems.at[slot, i]
            )
            for i, w in enumerate((gate_weight, up_weight))
        ]

    for c in range(2):
        for copy in weight_copies(c, forward_w, forward_sem):
            copy.start()
        for copy in weight_copies(c, backward_w, backward_sem):
            copy.start()

    barrier = pltpu.get_barrier_semaphore()
    for k in (1, 2, 3):
        pl.semaphore_signal(barrier, inc=1, device_id={"wt": plane[k]}, device_id_type=MESH)
    pl.semaphore_signal(barrier, inc=1, device_id=core, device_id_type=MESH)
    pl.semaphore_signal(barrier, inc=1, device_id={"inp": paired}, device_id_type=MESH)

    @pl.when(is_mid)
    def _():
        pl.semaphore_signal(barrier, inc=1, device_id={"inp": other_mid}, device_id_type=MESH)
        pl.semaphore_wait(barrier, 6)

    @pl.when(is_edge)
    def _():
        pl.semaphore_wait(barrier, 5)

    def block(w, o):
        return pl.ds(pl.multiple_of((w * 2 + o) * rows, rows), rows)

    mine = block(wt, out)
    gathers = [remote(tokens, features.at[mine], gather_send.at[0], gather_recv.at[0], core)]
    for k in (3, 1, 2):
        gathers.append(
            remote(tokens, features.at[mine], gather_send.at[k], gather_recv.at[k], {"wt": plane[k]})
        )
    for copy in gathers:
        copy.start()

    @pl.when(is_edge)
    def _():
        remote(hidden, grads.at[z], grad_send.at[0], grad_recv.at[0], {"inp": paired}).start()

    @pl.when(is_mid)
    def _():
        remote(hidden, grads.at[z], grad_send.at[0], grad_recv.at[1], {"inp": other_mid}).start()
        grads[z] = hidden[...]

    features[mine, :] = tokens[...]
    total[...] = jnp.zeros_like(total)

    relays = []
    for k in (1, 2, 3):
        theirs = block(plane[k], out)
        remote(
            tokens, features.at[theirs], gather_send.at[k], gather_recv.at[k], {"wt": plane[k]}
        ).wait_recv()
        relay = remote(
            features.at[theirs], features.at[theirs], relay_send.at[k], relay_recv.at[k], core
        )
        relay.start()
        relays.append(relay)

    def relayed_grads():
        return remote(
            grads.at[paired], grads.at[paired], grad_send.at[1], grad_recv.at[2], {"inp": other_mid}
        )

    @pl.when(is_mid)
    def _():
        remote(
            hidden, grads.at[paired], grad_send.at[0], grad_recv.at[0], {"inp": paired}
        ).wait_recv()
        relayed_grads().start()

    remote(
        tokens, features.at[block(wt, 1 - out)], gather_send.at[0], gather_recv.at[0], core
    ).wait_recv()
    for k in (1, 2, 3):
        theirs = block(plane[k], 1 - out)
        remote(
            features.at[theirs], features.at[theirs], relay_send.at[k], relay_recv.at[k], core
        ).wait_recv()
    features_copy = pltpu.make_async_copy(features, features_out, out_sem.at[0])
    features_copy.start()

    def edge_copy(c):
        return remote(
            acts_out.at[c], from_edge.at[c], act_send.at[c], edge_recv.at[c], {"inp": paired}
        )

    def mid_copy(c):
        return remote(
            acts_out.at[c], from_mid.at[c], act_send.at[c], mid_recv.at[c], {"inp": other_mid}
        )

    def delta_copy(c):
        return remote(
            delta.at[c], delta.at[c], delta_send.at[c], delta_recv.at[c], {"inp": paired}
        )

    def step(t, carry):
        @pl.when(t < chunks)
        def _():
            for copy in weight_copies(t, forward_w, forward_sem):
                copy.wait()
            partial = jnp.dot(
                features[...], forward_w[lax.rem(t, 2)], preferred_element_type=jnp.float32
            )

            @pl.when(is_edge)
            def _():
                acts_out[t] = partial.astype(jnp.bfloat16)
                edge_copy(t).start()

            @pl.when(is_mid)
            def _():
                own[t] = partial

            @pl.when(t + 2 < chunks)
            def _():
                for copy in weight_copies(t + 2, forward_w, forward_sem):
                    copy.start()

        c1 = t - SUM_LAG

        @pl.when(is_mid & (c1 >= 0) & (c1 < chunks))
        def _():
            edge_copy(c1).wait_recv()
            both = own[c1] + from_edge[c1].astype(jnp.float32)
            own[c1] = both
            acts_out[c1] = both.astype(jnp.bfloat16)
            mid_copy(c1).start()

        cb = t - jnp.where(is_mid, MID_LAG, EDGE_LAG)

        @pl.when((cb >= 0) & (cb < chunks))
        def _():
            @pl.when(is_edge)
            def _():
                delta_copy(cb).wait_recv()

            for copy in weight_copies(cb, backward_w, backward_sem):
                copy.wait()
            slot = lax.rem(cb, 2)

            def piece(i, carry):
                at = pl.ds(pl.multiple_of(i * 512, 512), 512)
                total[:, at] += lax.dot_general(
                    delta[cb], backward_w[slot, at, :], OVER_HIDDEN,
                    preferred_element_type=jnp.float32,
                )
                return carry

            lax.fori_loop(0, width // 512, piece, 0)

            @pl.when(cb + 2 < chunks)
            def _():
                for copy in weight_copies(cb + 2, backward_w, backward_sem):
                    copy.start()

        c2 = t - DELTA_LAG

        @pl.when(is_mid & (c2 == 0))
        def _():
            remote(
                hidden, grads.at[other_mid], grad_send.at[0], grad_recv.at[1], {"inp": other_mid}
            ).wait_recv()
            far = 3 - paired
            remote(
                grads.at[far], grads.at[far], grad_send.at[1], grad_recv.at[2], {"inp": other_mid}
            ).wait_recv()

        @pl.when(is_mid & (c2 >= 0) & (c2 < chunks))
        def _():
            mid_copy(c2).wait_recv()
            columns = pl.ds(pl.multiple_of(c2 * CHUNK, CHUNK), CHUNK)
            for q in range(4):
                part = pl.ds(q * chunk_rows, chunk_rows)
                acts = own[c2, part, :] + from_mid[c2, part, :].astype(jnp.float32)
                gate_delta, up_delta = deltas(
                    acts[:, :CHUNK], acts[:, CHUNK:], grads[q, :, columns].astype(jnp.float32)
                )
                delta[c2, part, pl.ds(0, CHUNK)] = gate_delta
                delta[c2, part, pl.ds(CHUNK, CHUNK)] = up_delta
            delta_copy(c2).start()

        return carry

    lax.fori_loop(0, chunks + EDGE_LAG, step, 0)
    delta_out_copy = pltpu.make_async_copy(delta, delta_out, out_sem.at[1])
    delta_out_copy.start()

    targets = (wt,) + plane[1:]

    def pair_copy(k, o):
        return remote(
            total.at[block(targets[k], o)], pair_in.at[k], pair_send.at[k], pair_recv.at[k], core
        )

    for k in (3, 1, 2, 0):
        pair_copy(k, 1 - out).start()
    for k in (3, 1, 2):
        pair_copy(k, 1 - out).wait_recv()
        plane_out[k - 1] = (total[block(targets[k], out), :] + pair_in[k]).astype(jnp.bfloat16)
        remote(
            plane_out.at[k - 1], plane_in.at[k - 1], plane_send.at[k], plane_recv.at[k],
            {"wt": plane[k]},
        ).start()
    pair_copy(0, 1 - out).wait_recv()
    result = total[mine, :] + pair_in[0]
    for k in (1, 2, 3):
        copy = remote(
            plane_out.at[k - 1], plane_in.at[k - 1], plane_send.at[k], plane_recv.at[k],
            {"wt": plane[k]},
        )
        copy.wait_recv()
        result = result + plane_in[k - 1].astype(jnp.float32)
        copy.wait_send()
    input_grad[...] = result.astype(jnp.bfloat16)

    for k in range(4):
        pair_copy(k, 1 - out).wait_send()
    for copy in gathers + relays:
        copy.wait_send()
    remote(hidden, grads.at[z], grad_send.at[0], grad_recv.at[0], {"inp": paired}).wait_send()

    @pl.when(is_mid)
    def _():
        relayed_grads().wait_send()

    def finish(c, carry):
        edge_copy(c).wait_send()

        @pl.when(is_mid)
        def _():
            delta_copy(c).wait_send()

        return carry

    lax.fori_loop(0, chunks, finish, 0)
    features_copy.wait()
    delta_out_copy.wait()


def exchange(tokens, gate_weight, up_weight, hidden_grad):
    rows, width = tokens.shape
    hidden = gate_weight.shape[1]
    chunks = hidden // CHUNK
    whole = rows * 8
    bf16, f32 = jnp.bfloat16, jnp.float32
    dma = pltpu.SemaphoreType.DMA
    vmem, hbm = pl.BlockSpec(memory_space=pltpu.VMEM), pl.BlockSpec(memory_space=pl.ANY)
    acts = (chunks, whole, 2 * CHUNK)
    return pl.pallas_call(
        functools.partial(exchange_kernel, chunks),
        out_shape=(
            jax.ShapeDtypeStruct((rows, width), bf16),
            jax.ShapeDtypeStruct((whole, width), bf16),
            jax.ShapeDtypeStruct(acts, bf16),
        ),
        in_specs=[vmem, vmem, hbm, hbm],
        out_specs=(vmem, hbm, hbm),
        scratch_shapes=[
            pltpu.VMEM((whole, width), bf16),
            pltpu.VMEM((4, whole // 4, hidden), bf16),
            pltpu.VMEM((2, width, 2 * CHUNK), bf16),
            pltpu.VMEM((2, width, 2 * CHUNK), bf16),
            pltpu.VMEM(acts, bf16),
            pltpu.VMEM(acts, bf16),
            pltpu.VMEM(acts, bf16),
            pltpu.VMEM(acts, bf16),
            pltpu.VMEM(acts, f32),
            pltpu.VMEM((whole, width), f32),
            pltpu.VMEM((4, rows, width), f32),
            pltpu.VMEM((3, rows, width), bf16),
            pltpu.VMEM((3, rows, width), bf16),
            dma((4,)), dma((4,)), dma((4,)), dma((4,)), dma((2,)), dma((3,)),
            dma((2, 2)), dma((2, 2)),
            dma((chunks,)), dma((chunks,)), dma((chunks,)), dma((chunks,)), dma((chunks,)),
            dma((4,)), dma((4,)), dma((4,)), dma((4,)), dma((2,)),
        ],
        compiler_params=pltpu.CompilerParams(
            collective_id=0, has_side_effects=True, vmem_limit_bytes=58 * 2**20
        ),
        cost_estimate=pl.CostEstimate(
            flops=8 * whole * width * hidden,
            bytes_accessed=8 * width * hidden,
            transcendentals=whole * hidden,
        ),
    )(tokens, hidden_grad, gate_weight, up_weight)


def chunk_grads_kernel(features, delta, gate_grad, up_grad, gate_delta, up_delta):
    @pl.when(pl.program_id(0) == 0)
    def _():
        for c in range(delta.shape[0]):
            at = pl.ds(c * CHUNK, CHUNK)
            gate_delta[:, at] = delta[c, :, pl.ds(0, CHUNK)]
            up_delta[:, at] = delta[c, :, pl.ds(CHUNK, CHUNK)]

    grads_kernel(features, gate_delta, up_delta, gate_grad, up_grad)


def chunk_grads(features, delta):
    tokens, width = features.shape
    chunks = delta.shape[0]
    hidden = chunks * CHUNK
    rows = 256
    grad = jax.ShapeDtypeStruct((width, hidden), jnp.bfloat16)
    return pl.pallas_call(
        chunk_grads_kernel,
        grid=(width // rows,),
        in_specs=[
            pl.BlockSpec((tokens, rows), lambda i: (0, i)),
            pl.BlockSpec(delta.shape, lambda i: (0, 0, 0)),
        ],
        out_specs=[pl.BlockSpec((rows, hidden), lambda i: (i, 0))] * 2,
        out_shape=[grad, grad],
        scratch_shapes=[pltpu.VMEM((tokens, hidden), jnp.bfloat16)] * 2,
        compiler_params=pltpu.CompilerParams(vmem_limit_bytes=40 * 2**20),
        cost_estimate=pl.CostEstimate(
            flops=4 * tokens * width * hidden,
            bytes_accessed=4 * width * hidden,
            transcendentals=0,
        ),
    )(features, delta)


def on_line(tokens, gate_weight, up_weight, hidden_grad):
    input_grad, features, delta = exchange(tokens, gate_weight, up_weight, hidden_grad)
    gate_grad, up_grad = chunk_grads(features, delta)
    return (input_grad, gate_grad, up_grad)


def solution(mesh):
    line = (mesh.shape["inp"], mesh.shape["wt"], mesh.shape["out"]) == (4, 4, 2)
    return jax.shard_map(
        on_line if line else per_device,
        mesh=mesh,
        in_specs=(
            P(("wt", "out"), "inp"),
            P("inp", ("wt", "out")),
            P("inp", ("wt", "out")),
            P("inp", ("wt", "out")),
        ),
        out_specs=(P(("wt", "out"), "inp"), P("inp", ("wt", "out")), P("inp", ("wt", "out"))),
        check_vma=False,
    )
```
